256 devices in a mesh: rows: 16 (over z, x_hi), cols: 16 (over x_lo, y, core).
Axes of the slice: x: 4 (x_hi: 2, x_lo: 2; x = x_hi * 2 + x_lo), y: 4, z: 8, core: 2. Of those that a mesh axis runs over, the one named last changes fastest.
Arguments:
- tokens: bfloat16 [1024, 1536, 144], P('rows', 'cols'), may hold values from -6 to 6
- norm1_gain: float32 [144], replicated, may hold values from 0.1 to 1.9
- norm1_bias: float32 [144], replicated, may hold values from -2.5 to 2.5
- qkv_weight: bfloat16 [144, 432], replicated, may hold values from -1.175 to 1.175
- qkv_bias: float32 [432], replicated, may hold values from -2.5 to 2.5
- lepe_taps: float32 [3, 144], replicated, may hold values from -3 to 3
- lepe_bias: float32 [144], replicated, may hold values from -2.5 to 2.5
- proj_weight: bfloat16 [144, 144], replicated, may hold values from -0.5 to 0.5
- proj_bias: float32 [144], replicated, may hold values from -2.5 to 2.5
- norm2_gain: float32 [144], replicated, may hold values from 0.1 to 1.9
- norm2_bias: float32 [144], replicated, may hold values from -2.5 to 2.5
- fc1_weight: bfloat16 [144, 576], replicated, may hold values from -0.5 to 0.5
- fc1_bias: float32 [576], replicated, may hold values from -2.5 to 2.5
- fc2_weight: bfloat16 [576, 144], replicated, may hold values from -0.25 to 0.25
- fc2_bias: float32 [144], replicated, may hold values from -2.5 to 2.5
Outputs:
- block_out: bfloat16 [1024, 1536, 144], P('rows', 'cols')
The draws below stay inside these ranges and needn't reach their ends.
All inputs are finite; a program needn't handle non-finite values.
Results may differ from the reference program's by a relative error of at most 0.003.
The reference program's roundings to bfloat16 on the way count: a program that leaves them out, or rounds other values in their place, can miss the bound.
Values may be sent and summed in bfloat16 or wider, within the bound.
A program may use at most 128 MiB of HBM per device.

```python
import math
import jax
import jax.numpy as jnp
from jax import lax

C = 144
FFN = 576
H = 1024
W = 1536


def draw_qkv_weight(key, part):
    key = jax.random.fold_in(key, 11)
    values = jax.random.normal(key, (C, 3 * C), jnp.float32)
    return (jnp.clip(values, -6.0, 6.0) * C ** (-0.5)).astype(jnp.bfloat16)


def block_scale(key, dims, pieces, least, top_value):
    level = 1.0
    for position, shards_of in pieces:
        steps = jax.random.uniform(jax.random.fold_in(jax.random.fold_in(key, 6), position), (shards_of,), jnp.float32, least / len(pieces), top_value / len(pieces))
        level = level * jnp.repeat(jnp.exp(steps), dims[position] // shards_of).reshape((-1,) + (1,) * (len(dims) - 1 - position))
    return level


def scatter_about(stream_key, shape, scale, limit, cuts=(), dtype=jnp.bfloat16):
    values = jax.random.normal(stream_key, shape, jnp.float32) * scale
    if len(cuts) > 0:
        values = block_scale(stream_key, shape, cuts, -0.22, 0.18) * values
    return jnp.clip(values, min=-limit, max=limit).astype(dtype)


def setup_inputs(seed: int = 0) -> dict:
    key_of = jax.random.split(jax.random.key(seed), 16)
    tokens = scatter_about(key_of[0], (H, W, C), 1.0, 6.0, ((0, 16), (1, 16)))
    norm1_gain = jnp.clip(1.0 + 0.18 * jax.random.normal(key_of[1], (C,), jnp.float32), 0.1, 1.9)
    norm1_bias = scatter_about(key_of[2], (C,), 0.4, 2.5, (), jnp.float32)
    qkv_weight = draw_qkv_weight(jax.random.fold_in(key_of[15], 71), 0)
    qkv_bias = scatter_about(key_of[4], (3 * C,), 0.4, 2.5, (), jnp.float32)
    lepe_taps = scatter_about(key_of[5], (3, C), 0.5, 3.0, (), jnp.float32)
    lepe_bias = scatter_about(key_of[6], (C,), 0.4, 2.5, (), jnp.float32)
    proj_weight = scatter_about(key_of[7], (C, C), C ** -0.5, 0.5)
    proj_bias = scatter_about(key_of[8], (C,), 0.4, 2.5, (), jnp.float32)
    norm2_gain = jnp.clip(1.0 + 0.18 * jax.random.normal(key_of[9], (C,), jnp.float32), 0.1, 1.9)
    norm2_bias = scatter_about(key_of[10], (C,), 0.4, 2.5, (), jnp.float32)
    fc1_weight = scatter_about(key_of[11], (C, FFN), C ** -0.5, 0.5)
    fc1_bias = scatter_about(key_of[12], (FFN,), 0.4, 2.5, (), jnp.float32)
    fc2_weight = scatter_about(key_of[13], (FFN, C), FFN ** -0.5, 0.25)
    fc2_bias = scatter_about(key_of[14], (C,), 0.4, 2.5, (), jnp.float32)
    return {"tokens": tokens, "norm1_gain": norm1_gain, "norm1_bias": norm1_bias, "qkv_weight": qkv_weight, "qkv_bias": qkv_bias, "lepe_taps": lepe_taps, "lepe_bias": lepe_bias, "proj_weight": proj_weight, "proj_bias": proj_bias, "norm2_gain": norm2_gain, "norm2_bias": norm2_bias, "fc1_weight": fc1_weight, "fc1_bias": fc1_bias, "fc2_weight": fc2_weight, "fc2_bias": fc2_bias}


def layer_norm(values, gain, bias):
    mean = lax.optimization_barrier(jnp.mean(values, axis=-1, keepdims=True))
    centred = values - mean
    variance = lax.optimization_barrier(jnp.mean(centred * centred, axis=-1, keepdims=True))
    return centred * lax.rsqrt(variance + 1e-05) * gain + bias

def stripe_attention(queries, keys, values):
    count, length, width = queries.shape
    heads = 3
    head_dim = width // heads
    block = math.gcd(length, 256)
    scale = head_dim ** (-0.5)
    q_blocks = queries.reshape(count, length // block, block, heads, head_dim)
    k_all = keys.reshape(count, length, heads, head_dim)
    v_all = values.reshape(count, length, heads, head_dim)

    def one_sequence(items):
        q_seq, k_seq, v_seq = items

        def one_block(q_block):
            scores = jnp.einsum('qhd,khd->hqk', q_block.astype(jnp.float32), k_seq.astype(jnp.float32)) * scale
            top = lax.optimization_barrier(jnp.max(scores, axis=-1, keepdims=True))
            expo = jnp.exp(scores - top)
            probs = (expo / lax.optimization_barrier(jnp.sum(expo, axis=-1, keepdims=True))).astype(jnp.bfloat16)
            out = jnp.einsum('hqk,khd->qhd', probs.astype(jnp.float32), v_seq.astype(jnp.float32))
            return out.reshape(block, width)
        return lax.map(one_block, q_seq).reshape(length, width)
    return lax.map(one_sequence, (q_blocks, k_all, v_all))

def reference(tokens, norm1_gain, norm1_bias, qkv_weight, qkv_bias, lepe_taps, lepe_bias, proj_weight, proj_bias, norm2_gain, norm2_bias, fc1_weight, fc1_bias, fc2_weight, fc2_bias):
    height, width, chans = tokens.shape
    half = chans // 2
    tok_f = tokens.astype(jnp.float32)
    normed = layer_norm(tok_f, norm1_gain, norm1_bias).astype(jnp.bfloat16)
    qkv = (jnp.dot(normed.reshape(-1, chans), qkv_weight, preferred_element_type=jnp.float32) + qkv_bias).astype(jnp.bfloat16)
    qkv = qkv.reshape(height, width, 3 * chans)
    q_all = qkv[..., :chans]
    k_all = qkv[..., chans:2 * chans]
    v_all = qkv[..., 2 * chans:]
    row_att = stripe_attention(q_all[..., :half], k_all[..., :half], v_all[..., :half]).astype(jnp.bfloat16)
    col_att = stripe_attention(jnp.swapaxes(q_all[..., half:], 0, 1), jnp.swapaxes(k_all[..., half:], 0, 1), jnp.swapaxes(v_all[..., half:], 0, 1)).astype(jnp.bfloat16)
    col_att = jnp.swapaxes(col_att, 0, 1)
    v_row = jnp.pad(v_all[..., :half].astype(jnp.float32), ((0, 0), (1, 1), (0, 0)))
    lepe_row = lepe_taps[0, :half] * v_row[:, :-2] + lepe_taps[1, :half] * v_row[:, 1:-1] + lepe_taps[2, :half] * v_row[:, 2:] + lepe_bias[:half]
    v_col = jnp.pad(v_all[..., half:].astype(jnp.float32), ((1, 1), (0, 0), (0, 0)))
    lepe_col = lepe_taps[0, half:] * v_col[:-2] + lepe_taps[1, half:] * v_col[1:-1] + lepe_taps[2, half:] * v_col[2:] + lepe_bias[half:]
    mixed_row = (row_att.astype(jnp.float32) + lepe_row).astype(jnp.bfloat16)
    mixed_col = (col_att.astype(jnp.float32) + lepe_col).astype(jnp.bfloat16)
    mixed = jnp.concatenate([mixed_row, mixed_col], axis=-1).reshape(-1, chans)
    resid = tok_f.reshape(-1, chans) + jnp.dot(mixed, proj_weight, preferred_element_type=jnp.float32) + proj_bias
    normed2 = layer_norm(resid, norm2_gain, norm2_bias).astype(jnp.bfloat16)
    hidden = jax.nn.gelu(jnp.dot(normed2, fc1_weight, preferred_element_type=jnp.float32) + fc1_bias, approximate=False).astype(jnp.bfloat16)
    block_out = resid + jnp.dot(hidden, fc2_weight, preferred_element_type=jnp.float32) + fc2_bias
    return block_out.astype(jnp.bfloat16).reshape(height, width, chans)
```

```python
import functools
import math

import jax
import jax.numpy as jnp
from jax import lax
from jax.experimental import pallas as pl
from jax.experimental.pallas import tpu as pltpu
from jax.sharding import PartitionSpec as P

HEADS = 3
HEAD = 24
HALF = 72
LANES = 128
F32 = jnp.float32
BF16 = jnp.bfloat16
SCALE = HEAD ** (-0.5) * math.log2(math.e)
SAFE = 80.0
NT = (((1,), (1,)), ((), ()))
TN = (((0,), (0,)), ((), ()))
VMEM = pl.BlockSpec(memory_space=pltpu.VMEM)


def pack_kernel(x_ref, eye_ref, gain_ref, bias_ref, out_ref):
    groups, per, chans = x_ref.shape
    x = x_ref[...].reshape(groups * per, chans)
    x = lax.dot_general(eye_ref[...], x, NT, preferred_element_type=F32)
    mean = jnp.mean(x, axis=0, keepdims=True)
    centred = x - mean
    variance = jnp.mean(centred * centred, axis=0, keepdims=True)
    normed = centred * lax.rsqrt(variance + 1e-05) * gain_ref[...] + bias_ref[...]
    out_ref[0] = normed.astype(BF16)


def pack(tokens, gain, bias, peers):
    length, per, chans = tokens.shape
    groups = length // peers
    const = lambda i: (0, 0)
    return pl.pallas_call(
        pack_kernel,
        grid=(peers,),
        out_shape=jax.ShapeDtypeStruct((peers, chans, groups * per), BF16),
        in_specs=[
            pl.BlockSpec((groups, per, chans), lambda i: (i, 0, 0)),
            pl.BlockSpec((chans, chans), const),
            pl.BlockSpec((chans, 1), const),
            pl.BlockSpec((chans, 1), const),
        ],
        out_specs=pl.BlockSpec((1, chans, groups * per), lambda i: (i, 0, 0)),
        cost_estimate=pl.CostEstimate(
            flops=4 * length * per * chans * chans, bytes_accessed=5 * 10**6, transcendentals=0
        ),
        name="pack",
    )(tokens, jnp.eye(chans, dtype=BF16), gain.reshape(chans, 1), bias.reshape(chans, 1))


def stripe_kernel(
    n_seq, per, qb, x_ref, w_ref, b_ref, taps_ref, lb_ref, out_ref, q_s, k_s, vt_s, vf_s, m_s
):
    peers = x_ref.shape[0]
    length = peers * per
    lane = lax.broadcasted_iota(jnp.int32, (1, LANES), 1)
    own = [(lane >= h * HEAD) & (lane < (h + 1) * HEAD) for h in range(HEADS)]
    heads = (
        lax.broadcasted_iota(jnp.int32, (LANES, LANES), 0) // HEAD
        == lax.broadcasted_iota(jnp.int32, (LANES, LANES), 1)
    ).astype(BF16)

    def project(s, tops):
        y = lax.dot_general(x_ref[s], w_ref[...], TN, preferred_element_type=F32)
        y = (y + b_ref[...]).astype(BF16)
        new = []
        for part, top in enumerate(tops):
            piece = y[:, part * LANES : (part + 1) * LANES]
            norms = jnp.dot(piece * piece, heads, preferred_element_type=F32)
            new.append(jnp.maximum(top, jnp.max(norms, axis=0, keepdims=True)))
        for i in range(n_seq):
            rows = slice(i * per, (i + 1) * per)
            dst = pl.ds(pl.multiple_of(s * per, 16), per)
            q_s[i, dst, :] = y[rows, :LANES]
            k_s[i, dst, :] = y[rows, LANES : 2 * LANES]
            dst = pl.ds(pl.multiple_of(8 + s * per, 8), per)
            vf_s[i, dst, :] = y[rows, 2 * LANES :].astype(F32)
        return tuple(new)

    for i in range(n_seq):
        vf_s[i, :8, :] = jnp.zeros((8, LANES), F32)
        vf_s[i, 8 + length :, :] = jnp.zeros((8, LANES), F32)
    zero = jnp.zeros((1, LANES), F32)
    q_top, k_top = lax.fori_loop(0, peers, project, (zero, zero))
    bound = jnp.max(q_top * k_top) * (1.05 * SCALE * SCALE)

    def turn(i, _):
        vt = vf_s[i, 8 : 8 + length, :].T
        for h in range(HEADS):
            both = [vt[h * HEAD : (h + 1) * HEAD], jnp.ones((8, length), F32)]
            vt_s[i, h] = jnp.concatenate(both, axis=0).astype(BF16)
        return 0

    lax.fori_loop(0, n_seq, turn, 0)
    blocks = length // qb

    def block(shifted, t, _):
        i = t // blocks
        at = pl.multiple_of((t % blocks) * qb, qb)
        q = q_s[i, pl.ds(at, qb), :]
        k = k_s[i]
        parts = []
        for h in range(HEADS):
            qh = jnp.where(own[h], q, jnp.zeros_like(q))
            s = lax.dot_general(k, qh, NT, preferred_element_type=F32)
            if shifted:
                s = s - jnp.max(s, axis=0, keepdims=True)
            p = jnp.exp2(s * SCALE).astype(BF16)
            o = jnp.dot(vt_s[i, h], p, preferred_element_type=F32)
            parts.append(o[:HEAD] / o[HEAD : HEAD + 1])
        parts.append(jnp.zeros((LANES - HALF, qb), F32))
        att = jnp.concatenate(parts, axis=0).T.astype(BF16).astype(F32)
        lepe = (
            taps_ref[0:1] * vf_s[i, pl.ds(at + 7, qb), :]
            + taps_ref[1:2] * vf_s[i, pl.ds(at + 8, qb), :]
            + taps_ref[2:3] * vf_s[i, pl.ds(at + 9, qb), :]
            + lb_ref[...]
        )
        m_s[i, pl.ds(at, qb), :] = att + lepe
        return 0

    safe = bound < SAFE * SAFE

    @pl.when(safe)
    def _():
        lax.fori_loop(0, n_seq * blocks, functools.partial(block, False), 0)

    @pl.when(jnp.logical_not(safe))
    def _():
        lax.fori_loop(0, n_seq * blocks, functools.partial(block, True), 0)

    def send(d, _):
        x = m_s[:, pl.ds(pl.multiple_of(d * per, 16), per), :].reshape(n_seq * per, LANES)
        out_ref[d] = x.T[:HALF].astype(BF16)
        return 0

    lax.fori_loop(0, peers, send, 0)


def stripe(received, weight, bias, taps, lepe_bias, per, qb):
    peers, _, width = received.shape
    n_seq = width // per
    length = peers * per
    return pl.pallas_call(
        functools.partial(stripe_kernel, n_seq, per, qb),
        out_shape=jax.ShapeDtypeStruct((peers, HALF, width), BF16),
        in_specs=[VMEM] * 5,
        out_specs=VMEM,
        scratch_shapes=[
            pltpu.VMEM((n_seq, length, LANES), BF16),
            pltpu.VMEM((n_seq, length, LANES), BF16),
            pltpu.VMEM((n_seq, HEADS, 32, length), BF16),
            pltpu.VMEM((n_seq, length + 16, LANES), F32),
            pltpu.VMEM((n_seq, length, LANES), F32),
        ],
        compiler_params=pltpu.CompilerParams(vmem_limit_bytes=50 * 2**20),
        cost_estimate=pl.CostEstimate(
            flops=4 * HEADS * n_seq * length * length * 256,
            bytes_accessed=4 * 10**6,
            transcendentals=HEADS * n_seq * length * length,
        ),
        name="stripe",
    )(received, weight, bias, taps, lepe_bias)


def tail_kernel(
    x_ref, row_ref, col_ref, eye_ref, wr_ref, wc_ref, pb_ref, g_ref, b_ref,
    f1_ref, f1b_ref, f2_ref, f2b_ref, out_ref, col_s,
):
    rows, tile_w, chans = x_ref.shape
    peers, _, width = col_ref.shape
    tile_h = rows * peers
    per = width // tile_h

    @pl.when(pl.program_id(0) == 0)
    def _():
        for r in range(peers):
            y = lax.dot_general(col_ref[r], eye_ref[...], TN, preferred_element_type=F32)
            for j in range(per):
                col_s[pl.ds(r * per + j, tile_h, stride=tile_w), :] = y[j * tile_h : (j + 1) * tile_h]

    count = rows * tile_w
    at = pl.multiple_of(pl.program_id(0) * count, count)
    col = col_s[pl.ds(at, count), :].astype(BF16)
    resid = (
        x_ref[...].reshape(count, chans).astype(F32)
        + lax.dot_general(row_ref[0], wr_ref[...], TN, preferred_element_type=F32)
        + jnp.dot(col, wc_ref[...], preferred_element_type=F32)
        + pb_ref[...]
    )
    mean = jnp.mean(resid, axis=-1, keepdims=True)
    centred = resid - mean
    variance = jnp.mean(centred * centred, axis=-1, keepdims=True)
    normed = (centred * lax.rsqrt(variance + 1e-05) * g_ref[...] + b_ref[...]).astype(BF16)
    hidden = jnp.dot(normed, f1_ref[...], preferred_element_type=F32) + f1b_ref[...]
    hidden = (0.5 * hidden * (1.0 + lax.erf(hidden * (0.5**0.5)))).astype(BF16)
    out = resid + jnp.dot(hidden, f2_ref[...], preferred_element_type=F32) + f2b_ref[...]
    out_ref[...] = out.astype(BF16).reshape(rows, tile_w, chans)


def tail(tokens, row, col, proj_w, proj_b, gain, bias, fc1_w, fc1_b, fc2_w, fc2_b):
    tile_h, tile_w, chans = tokens.shape
    peers, _, width = row.shape
    rows = tile_h // peers
    ffn = fc1_w.shape[1]
    const2 = lambda i: (0, 0)
    full = lambda a: pl.BlockSpec(a.shape, lambda i: (0,) * a.ndim)
    wc = jnp.pad(proj_w[HALF:], ((0, LANES - HALF), (0, 0)))
    consts = [
        jnp.eye(HALF, LANES, dtype=BF16), proj_w[:HALF], wc, proj_b[None], gain[None], bias[None],
        fc1_w, fc1_b[None], fc2_w, fc2_b[None],
    ]
    return pl.pallas_call(
        tail_kernel,
        grid=(peers,),
        out_shape=jax.ShapeDtypeStruct(tokens.shape, BF16),
        in_specs=[
            pl.BlockSpec((rows, tile_w, chans), lambda i: (i, 0, 0)),
            pl.BlockSpec((1, HALF, width), lambda i: (i, 0, 0)),
            full(col),
        ] + [full(a) for a in consts],
        out_specs=pl.BlockSpec((rows, tile_w, chans), lambda i: (i, 0, 0)),
        scratch_shapes=[pltpu.VMEM((tile_h * tile_w, LANES), F32)],
        compiler_params=pltpu.CompilerParams(vmem_limit_bytes=50 * 2**20),
        cost_estimate=pl.CostEstimate(
            flops=2 * tile_h * tile_w * chans * (chans + 2 * ffn),
            bytes_accessed=8 * 10**6,
            transcendentals=tile_h * tile_w * ffn,
        ),
        name="tail",
    )(tokens, row, col, *consts)


def shards(
    tokens, norm1_gain, norm1_bias, qkv_weight, qkv_bias, lepe_taps, lepe_bias, proj_weight,
    proj_bias, norm2_gain, norm2_bias, fc1_weight, fc1_bias, fc2_weight, fc2_bias,
):
    tile_h, tile_w, chans = tokens.shape
    n_rows = lax.axis_size("rows")
    n_cols = lax.axis_size("cols")

    def branch(which):
        lo = which * HALF
        lanes = lambda a: jnp.pad(a, [(0, 0)] * (a.ndim - 1) + [(0, LANES - HALF)])
        cut = lambda a: jnp.concatenate(
            [lanes(a[..., b * chans + lo : b * chans + lo + HALF]) for b in range(3)], axis=-1
        )
        return (
            cut(qkv_weight),
            cut(qkv_bias)[None],
            lanes(lepe_taps[:, lo : lo + HALF]),
            lanes(lepe_bias[lo : lo + HALF])[None],
        )

    swap = lambda a, axis: lax.all_to_all(a, axis, split_axis=0, concat_axis=0, tiled=True)
    row_in = swap(pack(tokens, norm1_gain, norm1_bias, n_cols), "cols")
    col_in = swap(pack(jnp.swapaxes(tokens, 0, 1), norm1_gain, norm1_bias, n_rows), "rows")
    row_out = swap(stripe(row_in, *branch(0), tile_w, 768), "cols")
    col_out = swap(stripe(col_in, *branch(1), tile_h, 1024), "rows")
    return tail(
        tokens, row_out, col_out, proj_weight, proj_bias, norm2_gain, norm2_bias,
        fc1_weight, fc1_bias, fc2_weight, fc2_bias,
    )


def solution(mesh):
    in_specs = (P("rows", "cols", None),) + (P(),) * 14
    return jax.shard_map(
        shards, mesh=mesh, in_specs=in_specs, out_specs=P("rows", "cols", None), check_vma=False
    )
```

```python
import functools
import math

import jax
import jax.numpy as jnp
from jax import lax
from jax.experimental import pallas as pl
from jax.experimental.pallas import tpu as pltpu
from jax.sharding import PartitionSpec as P

HEADS = 3
HEAD = 24
HALF = 72
LANES = 128
F32 = jnp.float32
BF16 = jnp.bfloat16
SCALE = HEAD ** (-0.5) * math.log2(math.e)
SAFE = 80.0
UNROLL = 4
NT = (((1,), (1,)), ((), ()))
TN = (((0,), (0,)), ((), ()))
VMEM = pl.BlockSpec(memory_space=pltpu.VMEM)


def columns(row, lanes):
    return jnp.broadcast_to(row, (lanes, row.shape[1])).T


def norm_channels(x, gain, bias):
    mean = jnp.mean(x, axis=0, keepdims=True)
    centred = x - mean
    variance = jnp.mean(centred * centred, axis=0, keepdims=True)
    return centred * lax.rsqrt(variance + 1e-05) * gain + bias


def pack_rows_kernel(x_ref, gain_ref, bias_ref, out_ref):
    rows, chans, cols = x_ref.shape
    gain = columns(gain_ref[...], cols)
    bias = columns(bias_ref[...], cols)
    peers = out_ref.shape[0]
    each = rows // peers

    def turn(p, _):
        xs = [
            norm_channels(x_ref[p * each + i].astype(F32), gain, bias) for i in range(each)
        ]
        out_ref[p] = jnp.concatenate(xs, axis=1).astype(BF16)
        return 0

    lax.fori_loop(0, peers, turn, 0, unroll=2)


def pack_cols_kernel(x_ref, gain_ref, bias_ref, out_ref, turned):
    rows, chans, cols = x_ref.shape
    peers, _, width = out_ref.shape
    spot = lambda shape: lax.broadcasted_iota(jnp.int32, shape, 0) == lax.broadcasted_iota(
        jnp.int32, shape, 1
    )
    wide = spot((chans, 2 * LANES)).astype(BF16)
    eye = spot((chans, chans)).astype(BF16)
    gain = columns(gain_ref[...], cols)
    bias = columns(bias_ref[...], cols)
    step = 16

    def turn(g, _):
        ys = []
        for i in range(step):
            x = norm_channels(x_ref[g * step + i].astype(F32), gain, bias)
            ys.append(lax.dot_general(x.astype(BF16), wide, TN, preferred_element_type=F32))
        at = pl.ds(pl.multiple_of(g * step, step), step)
        turned[:, at, :] = jnp.swapaxes(jnp.stack(ys), 0, 1)
        return 0

    lax.fori_loop(0, rows // step, turn, 0)
    per = width // rows

    def write(p, _):
        x = turned[pl.ds(p * per, per)].reshape(width, 2 * LANES)[:, :chans].astype(BF16)
        out = lax.dot_general(eye, x, NT, preferred_element_type=F32)
        out_ref[p] = out.astype(BF16)
        return 0

    lax.fori_loop(0, peers, write, 0, unroll=4)


def pack(kernel, scratch, name, tokens, gain, bias, peers):
    rows, chans, cols = tokens.shape
    return pl.pallas_call(
        kernel,
        out_shape=jax.ShapeDtypeStruct((peers, chans, rows * cols // peers), BF16),
        in_specs=[VMEM] * 3,
        out_specs=VMEM,
        scratch_shapes=scratch,
        compiler_params=pltpu.CompilerParams(vmem_limit_bytes=40 * 2**20),
        cost_estimate=pl.CostEstimate(
            flops=10**10, bytes_accessed=5 * 10**6, transcendentals=0
        ),
        name=name,
    )(tokens, gain[None], bias[None])


def stripe_kernel(
    first, n_seq, per, qb, x_ref, w_ref, b_ref, taps_ref, lb_ref, out_ref,
    q_s, k_s, vt_s, vf_s, m_s,
):
    peers = x_ref.shape[0]
    length = peers * per
    lane = lax.broadcasted_iota(jnp.int32, (1, LANES), 1)
    own = [(lane >= h * HEAD) & (lane < (h + 1) * HEAD) for h in range(HEADS)]
    heads = (
        lax.broadcasted_iota(jnp.int32, (LANES, LANES), 0) // HEAD
        == lax.broadcasted_iota(jnp.int32, (LANES, LANES), 1)
    ).astype(BF16)

    def project(s, tops):
        x = x_ref[s][:, first * per : (first + n_seq) * per]
        y = lax.dot_general(x, w_ref[...], TN, preferred_element_type=F32)
        y = (y + b_ref[...]).astype(BF16)
        new = []
        for part, top in enumerate(tops):
            piece = y[:, part * LANES : (part + 1) * LANES]
            norms = jnp.dot(piece * piece, heads, preferred_element_type=F32)
            new.append(jnp.maximum(top, jnp.max(norms, axis=0, keepdims=True)))
        for i in range(n_seq):
            rows = slice(i * per, (i + 1) * per)
            dst = pl.ds(pl.multiple_of(s * per, 16), per)
            q_s[i, dst, :] = y[rows, :LANES]
            k_s[i, dst, :] = y[rows, LANES : 2 * LANES]
            dst = pl.ds(pl.multiple_of(8 + s * per, 8), per)
            vf_s[i, dst, :] = y[rows, 2 * LANES :].astype(F32)
        return tuple(new)

    for i in range(n_seq):
        vf_s[i, :8, :] = jnp.zeros((8, LANES), F32)
        vf_s[i, 8 + length :, :] = jnp.zeros((8, LANES), F32)
    zero = jnp.zeros((1, LANES), F32)
    q_top, k_top = lax.fori_loop(0, peers, project, (zero, zero), unroll=UNROLL)
    bound = jnp.max(q_top * k_top) * (1.05 * SCALE * SCALE)

    def turn(i, _):
        vt = vf_s[i, 8 : 8 + length, :].T
        for h in range(HEADS):
            both = [vt[h * HEAD : (h + 1) * HEAD], jnp.ones((8, length), F32)]
            vt_s[i, h] = jnp.concatenate(both, axis=0).astype(BF16)
        return 0

    lax.fori_loop(0, n_seq, turn, 0)
    blocks = length // qb

    def block(shifted, t, _):
        i = t // blocks
        at = pl.multiple_of((t % blocks) * qb, qb)
        q = q_s[i, pl.ds(at, qb), :]
        k = k_s[i]
        parts = []
        for h in range(HEADS):
            qh = jnp.where(own[h], q, jnp.zeros_like(q))
            s = lax.dot_general(k, qh, NT, preferred_element_type=F32)
            if shifted:
                s = s - jnp.max(s, axis=0, keepdims=True)
            p = jnp.exp2(s * SCALE).astype(BF16)
            o = jnp.dot(vt_s[i, h], p, preferred_element_type=F32)
            parts.append(o[:HEAD] / o[HEAD : HEAD + 1])
        parts.append(jnp.zeros((LANES - HALF, qb), F32))
        att = jnp.concatenate(parts, axis=0).T.astype(BF16).astype(F32)
        lepe = (
            taps_ref[0:1] * vf_s[i, pl.ds(at + 7, qb), :]
            + taps_ref[1:2] * vf_s[i, pl.ds(at + 8, qb), :]
            + taps_ref[2:3] * vf_s[i, pl.ds(at + 9, qb), :]
            + lb_ref[...]
        )
        m_s[i, pl.ds(at, qb), :] = att + lepe
        return 0

    safe = bound < SAFE * SAFE

    @pl.when(safe)
    def _():
        lax.fori_loop(0, n_seq * blocks, functools.partial(block, False), 0)

    @pl.when(jnp.logical_not(safe))
    def _():
        lax.fori_loop(0, n_seq * blocks, functools.partial(block, True), 0)

    def send(d, _):
        at = pl.ds(pl.multiple_of(d * per, 16), per)
        out_ref[d] = m_s[:, at, :].reshape(n_seq * per, LANES).T[:HALF].astype(BF16)
        return 0

    lax.fori_loop(0, peers, send, 0, unroll=UNROLL)


def stripe(received, weight, bias, taps, lepe_bias, per, qb, first, n_seq):
    peers = received.shape[0]
    length = peers * per
    return pl.pallas_call(
        functools.partial(stripe_kernel, first, n_seq, per, qb),
        out_shape=jax.ShapeDtypeStruct((peers, HALF, n_seq * per), BF16),
        in_specs=[VMEM] * 5,
        out_specs=VMEM,
        scratch_shapes=[
            pltpu.VMEM((n_seq, length, LANES), BF16),
            pltpu.VMEM((n_seq, length, LANES), BF16),
            pltpu.VMEM((n_seq, HEADS, 32, length), BF16),
            pltpu.VMEM((n_seq, length + 16, LANES), F32),
            pltpu.VMEM((n_seq, length, LANES), F32),
        ],
        compiler_params=pltpu.CompilerParams(vmem_limit_bytes=44 * 2**20),
        cost_estimate=pl.CostEstimate(
            flops=4 * HEADS * n_seq * length * length * 256,
            bytes_accessed=4 * 10**6,
            transcendentals=HEADS * n_seq * length * length,
        ),
        name="stripe",
    )(received, weight, bias, taps, lepe_bias)


def tail_kernel(cuts, x_ref, row_ref, *refs):
    cols = refs[: len(cuts)]
    (eye_ref, wr_ref, wc_ref, vec_ref, f1_ref, f1b_ref, f2_ref, out_ref, col_s) = refs[len(cuts) :]
    rows, chans, tile_w = x_ref.shape
    each = row_ref.shape[2] // tile_w
    peers = cols[0].shape[0]
    tile_h = rows * pl.num_programs(0)
    per = tile_w // peers

    @pl.when(pl.program_id(0) == 0)
    def _():
        for (first, count), col_ref in zip(cuts, cols):
            for p in range(peers):
                y = lax.dot_general(col_ref[p], eye_ref[...], TN, preferred_element_type=F32)
                for j in range(count):
                    dst = pl.ds(p * per + first + j, tile_h, stride=tile_w)
                    col_s[dst, :] = y[j * tile_h : (j + 1) * tile_h]

    pb, gain, bias, f2b = [columns(vec_ref[i : i + 1], tile_w) for i in range(4)]
    resids, turned = [], []
    count = rows * tile_w
    both = col_s[pl.ds(pl.multiple_of(pl.program_id(0) * count, count), count), :].astype(BF16)
    for i in range(rows):
        col = both[i * tile_w : (i + 1) * tile_w]
        row = row_ref[i // each][:, i % each * tile_w : (i % each + 1) * tile_w]
        resid = (
            x_ref[i].astype(F32)
            + jnp.dot(wr_ref[...], row, preferred_element_type=F32)
            + lax.dot_general(wc_ref[...], col, NT, preferred_element_type=F32)
            + pb
        )
        turned.append(norm_channels(resid, gain, bias).T.astype(BF16))
        resids.append(resid + f2b)
    normed = jnp.concatenate(turned, axis=0)
    hidden = jnp.dot(normed, f1_ref[...], preferred_element_type=F32) + f1b_ref[...]
    hidden = (0.5 * hidden * (1.0 + lax.erf(hidden * (0.5**0.5)))).astype(BF16)
    out = jnp.dot(hidden, f2_ref[...], preferred_element_type=F32)
    for i in range(rows):
        piece = out[i * tile_w : (i + 1) * tile_w].T
        out_ref[i] = (resids[i] + piece).astype(BF16)


def tail(tokens, row, cuts, cols, proj_w, proj_b, gain, bias, fc1_w, fc1_b, fc2_w, fc2_b):
    tile_h, chans, tile_w = tokens.shape
    each = row.shape[2] // tile_w
    rows = 16 if 16 % each == 0 else each
    ffn = fc1_w.shape[1]
    full = lambda a: pl.BlockSpec(a.shape, lambda i: (0,) * a.ndim)
    block = lambda d: pl.BlockSpec((rows, d, tile_w), lambda i: (i, 0, 0))
    proj_t = proj_w.T
    consts = [
        jnp.eye(HALF, LANES, dtype=BF16), proj_t[:, :HALF],
        jnp.pad(proj_t[:, HALF:], ((0, 0), (0, LANES - HALF))),
        jnp.stack([proj_b, gain, bias, fc2_b]), fc1_w, fc1_b[None], fc2_w,
    ]
    return pl.pallas_call(
        functools.partial(tail_kernel, cuts),
        grid=(tile_h // rows,),
        out_shape=jax.ShapeDtypeStruct(tokens.shape, BF16),
        in_specs=[block(chans), pl.BlockSpec((rows // each,) + row.shape[1:], lambda i: (i, 0, 0))]
        + [full(a) for a in cols] + [full(a) for a in consts],
        out_specs=block(chans),
        scratch_shapes=[pltpu.VMEM((tile_h * tile_w, LANES), F32)],
        compiler_params=pltpu.CompilerParams(vmem_limit_bytes=44 * 2**20),
        cost_estimate=pl.CostEstimate(
            flops=2 * tile_h * tile_w * chans * (chans + 2 * ffn),
            bytes_accessed=8 * 10**6,
            transcendentals=tile_h * tile_w * ffn,
        ),
        name="tail",
    )(tokens, row, *cols, *consts)


def shards(
    tokens, norm1_gain, norm1_bias, qkv_weight, qkv_bias, lepe_taps, lepe_bias, proj_weight,
    proj_bias, norm2_gain, norm2_bias, fc1_weight, fc1_bias, fc2_weight, fc2_bias,
):
    tokens = jnp.swapaxes(tokens, 1, 2)
    tile_h, chans, tile_w = tokens.shape
    n_rows = lax.axis_size("rows")
    n_cols = lax.axis_size("cols")

    def branch(which):
        lo = which * HALF
        lanes = lambda a: jnp.pad(a, [(0, 0)] * (a.ndim - 1) + [(0, LANES - HALF)])
        cut = lambda a: jnp.concatenate(
            [lanes(a[..., b * chans + lo : b * chans + lo + HALF]) for b in range(3)], axis=-1
        )
        return (
            cut(qkv_weight),
            cut(qkv_bias)[None],
            lanes(lepe_taps[:, lo : lo + HALF]),
            lanes(lepe_bias[lo : lo + HALF])[None],
        )

    swap = lambda a, axis: lax.all_to_all(a, axis, split_axis=0, concat_axis=0, tiled=True)
    norm1 = (tokens, norm1_gain, norm1_bias)
    turned = [pltpu.VMEM((tile_w, tile_h, 2 * LANES), F32)]
    row_in = swap(pack(pack_rows_kernel, [], "pack_rows", *norm1, n_cols), "cols")
    col_in = swap(pack(pack_cols_kernel, turned, "pack_cols", *norm1, n_rows), "rows")
    rows = stripe(row_in, *branch(0), tile_w, n_cols * tile_w // 2, 0, tile_h // n_cols)
    rows = swap(rows, "cols")
    cuts = ((0, tile_w // n_rows),)
    cols = [
        swap(stripe(col_in, *branch(1), tile_h, n_rows * tile_h, *cut), "rows") for cut in cuts
    ]
    out = tail(
        tokens, rows, cuts, cols, proj_weight, proj_bias, norm2_gain, norm2_bias,
        fc1_weight, fc1_bias, fc2_weight, fc2_bias,
    )
    return jnp.swapaxes(out, 1, 2)


def solution(mesh):
    in_specs = (P("rows", "cols", None),) + (P(),) * 14
    return jax.shard_map(
        shards, mesh=mesh, in_specs=in_specs, out_specs=P("rows", "cols", None), check_vma=False
    )
```

```python
import functools
import math

import jax
import jax.numpy as jnp
from jax import lax
from jax.experimental import pallas as pl
from jax.experimental.pallas import tpu as pltpu
from jax.sharding import PartitionSpec as P

HEADS = 3
HEAD = 24
HALF = 72
LANES = 128
F32 = jnp.float32
BF16 = jnp.bfloat16
SCALE = HEAD ** (-0.5) * math.log2(math.e)
SAFE = 80.0
UNROLL = 4
NT = (((1,), (1,)), ((), ()))
TN = (((0,), (0,)), ((), ()))
VMEM = pl.BlockSpec(memory_space=pltpu.VMEM)
MESH = pl.DeviceIdType.MESH


def columns(row, lanes):
    return jnp.broadcast_to(row, (lanes, row.shape[1])).T


def norm_channels(x, gain, bias):
    mean = jnp.mean(x, axis=0, keepdims=True)
    centred = x - mean
    variance = jnp.mean(centred * centred, axis=0, keepdims=True)
    return centred * lax.rsqrt(variance + 1e-05) * gain + bias


def pack_rows_kernel(x_ref, gain_ref, bias_ref, out_ref):
    rows, chans, cols = x_ref.shape
    gain = columns(gain_ref[...], cols)
    bias = columns(bias_ref[...], cols)
    peers = out_ref.shape[0]
    each = rows // peers

    def turn(p, _):
        xs = [
            norm_channels(x_ref[p * each + i].astype(F32), gain, bias) for i in range(each)
        ]
        out_ref[p] = jnp.concatenate(xs, axis=1).astype(BF16)
        return 0

    lax.fori_loop(0, peers, turn, 0, unroll=2)


def pack_cols_kernel(x_ref, gain_ref, bias_ref, out_ref, turned):
    rows, chans, cols = x_ref.shape
    peers, _, width = out_ref.shape
    spot = lambda shape: lax.broadcasted_iota(jnp.int32, shape, 0) == lax.broadcasted_iota(
        jnp.int32, shape, 1
    )
    wide = spot((chans, 2 * LANES)).astype(BF16)
    eye = spot((chans, chans)).astype(BF16)
    gain = columns(gain_ref[...], cols)
    bias = columns(bias_ref[...], cols)
    step = 16

    def turn(g, _):
        ys = []
        for i in range(step):
            x = norm_channels(x_ref[g * step + i].astype(F32), gain, bias)
            ys.append(lax.dot_general(x.astype(BF16), wide, TN, preferred_element_type=F32))
        at = pl.ds(pl.multiple_of(g * step, step), step)
        turned[:, at, :] = jnp.swapaxes(jnp.stack(ys), 0, 1)
        return 0

    lax.fori_loop(0, rows // step, turn, 0)
    per = width // rows

    def write(p, _):
        x = turned[pl.ds(p * per, per)].reshape(width, 2 * LANES)[:, :chans].astype(BF16)
        out = lax.dot_general(eye, x, NT, preferred_element_type=F32)
        out_ref[p] = out.astype(BF16)
        return 0

    lax.fori_loop(0, peers, write, 0, unroll=4)


def pack(kernel, scratch, name, tokens, gain, bias, peers):
    rows, chans, cols = tokens.shape
    return pl.pallas_call(
        kernel,
        out_shape=jax.ShapeDtypeStruct((peers, chans, rows * cols // peers), BF16),
        in_specs=[VMEM] * 3,
        out_specs=VMEM,
        scratch_shapes=scratch,
        compiler_params=pltpu.CompilerParams(vmem_limit_bytes=40 * 2**20),
        cost_estimate=pl.CostEstimate(
            flops=10**10, bytes_accessed=5 * 10**6, transcendentals=0
        ),
        name=name,
    )(tokens, gain[None], bias[None])


def swap_kernel(axis, x_ref, out_ref, send_sem, recv_sem, own_sem):
    peers = lax.axis_size(axis)
    me = lax.axis_index(axis)
    barrier = pltpu.get_barrier_semaphore()

    def greet(k, _):
        peer = lax.rem(me + k, peers)
        pl.semaphore_signal(barrier, inc=1, device_id={axis: peer}, device_id_type=MESH)
        return 0

    lax.fori_loop(1, peers, greet, 0)
    pl.semaphore_wait(barrier, peers - 1)

    def copy(k):
        peer = lax.rem(me + k, peers)
        return pltpu.make_async_remote_copy(
            src_ref=x_ref.at[peer],
            dst_ref=out_ref.at[me],
            send_sem=send_sem.at[k],
            recv_sem=recv_sem.at[k],
            device_id={axis: peer},
            device_id_type=MESH,
        )

    def arrival(k):
        peer = lax.rem(me + peers - k, peers)
        return pltpu.make_async_remote_copy(
            src_ref=x_ref.at[peer],
            dst_ref=out_ref.at[peer],
            send_sem=send_sem.at[k],
            recv_sem=recv_sem.at[k],
            device_id={axis: peer},
            device_id_type=MESH,
        )

    def start(k, _):
        copy(k).start()
        return 0

    def finish(k, _):
        copy(k).wait_send()
        arrival(k).wait_recv()
        return 0

    lax.fori_loop(1, peers, start, 0)
    own = pltpu.make_async_copy(x_ref.at[me], out_ref.at[me], own_sem)
    own.start()
    own.wait()
    lax.fori_loop(1, peers, finish, 0)


def swap_blocks(x, axis, collective_id):
    peers = x.shape[0]
    return pl.pallas_call(
        functools.partial(swap_kernel, axis),
        out_shape=jax.ShapeDtypeStruct(x.shape, x.dtype),
        in_specs=[pl.BlockSpec(memory_space=pl.ANY)],
        out_specs=pl.BlockSpec(memory_space=pl.ANY),
        scratch_shapes=[
            pltpu.SemaphoreType.DMA((peers,)),
            pltpu.SemaphoreType.DMA((peers,)),
            pltpu.SemaphoreType.DMA,
        ],
        compiler_params=pltpu.CompilerParams(collective_id=collective_id, has_side_effects=True),
        cost_estimate=pl.CostEstimate(flops=2 * 10**10, bytes_accessed=4 * 10**6, transcendentals=0),
        name="swap_blocks",
    )(x)


def stripe_kernel(
    first, n_seq, per, qb, x_ref, w_ref, b_ref, taps_ref, lb_ref, out_ref,
    q_s, k_s, vt_s, vf_s, m_s,
):
    peers = x_ref.shape[0]
    length = peers * per
    lane = lax.broadcasted_iota(jnp.int32, (1, LANES), 1)
    own = [(lane >= h * HEAD) & (lane < (h + 1) * HEAD) for h in range(HEADS)]
    heads = (
        lax.broadcasted_iota(jnp.int32, (LANES, LANES), 0) // HEAD
        == lax.broadcasted_iota(jnp.int32, (LANES, LANES), 1)
    ).astype(BF16)

    def project(s, tops):
        x = x_ref[s][:, first * per : (first + n_seq) * per]
        y = lax.dot_general(x, w_ref[...], TN, preferred_element_type=F32)
        y = (y + b_ref[...]).astype(BF16)
        new = []
        for part, top in enumerate(tops):
            piece = y[:, part * LANES : (part + 1) * LANES]
            norms = jnp.dot(piece * piece, heads, preferred_element_type=F32)
            new.append(jnp.maximum(top, jnp.max(norms, axis=0, keepdims=True)))
        for i in range(n_seq):
            rows = slice(i * per, (i + 1) * per)
            dst = pl.ds(pl.multiple_of(s * per, 16), per)
            q_s[i, dst, :] = y[rows, :LANES]
            k_s[i, dst, :] = y[rows, LANES : 2 * LANES]
            dst = pl.ds(pl.multiple_of(8 + s * per, 8), per)
            vf_s[i, dst, :] = y[rows, 2 * LANES :].astype(F32)
        return tuple(new)

    for i in range(n_seq):
        vf_s[i, :8, :] = jnp.zeros((8, LANES), F32)
        vf_s[i, 8 + length :, :] = jnp.zeros((8, LANES), F32)
    zero = jnp.zeros((1, LANES), F32)
    q_top, k_top = lax.fori_loop(0, peers, project, (zero, zero), unroll=UNROLL)
    bound = jnp.max(q_top * k_top) * (1.05 * SCALE * SCALE)

    def turn(i, _):
        vt = vf_s[i, 8 : 8 + length, :].T
        for h in range(HEADS):
            both = [vt[h * HEAD : (h + 1) * HEAD], jnp.ones((8, length), F32)]
            vt_s[i, h] = jnp.concatenate(both, axis=0).astype(BF16)
        return 0

    lax.fori_loop(0, n_seq, turn, 0)
    blocks = length // qb

    def block(shifted, t, _):
        i = t // blocks
        at = pl.multiple_of((t % blocks) * qb, qb)
        q = q_s[i, pl.ds(at, qb), :]
        k = k_s[i]
        parts = []
        for h in range(HEADS):
            qh = jnp.where(own[h], q, jnp.zeros_like(q))
            s = lax.dot_general(k, qh, NT, preferred_element_type=F32)
            if shifted:
                s = s - jnp.max(s, axis=0, keepdims=True)
            p = jnp.exp2(s * SCALE).astype(BF16)
            o = jnp.dot(vt_s[i, h], p, preferred_element_type=F32)
            parts.append(o[:HEAD] / o[HEAD : HEAD + 1])
        parts.append(jnp.zeros((LANES - HALF, qb), F32))
        att = jnp.concatenate(parts, axis=0).T.astype(BF16).astype(F32)
        lepe = (
            taps_ref[0:1] * vf_s[i, pl.ds(at + 7, qb), :]
            + taps_ref[1:2] * vf_s[i, pl.ds(at + 8, qb), :]
            + taps_ref[2:3] * vf_s[i, pl.ds(at + 9, qb), :]
            + lb_ref[...]
        )
        m_s[i, pl.ds(at, qb), :] = att + lepe
        return 0

    safe = bound < SAFE * SAFE

    @pl.when(safe)
    def _():
        lax.fori_loop(0, n_seq * blocks, functools.partial(block, False), 0)

    @pl.when(jnp.logical_not(safe))
    def _():
        lax.fori_loop(0, n_seq * blocks, functools.partial(block, True), 0)

    def send(d, _):
        at = pl.ds(pl.multiple_of(d * per, 16), per)
        x = m_s[:, at, :].reshape(n_seq * per, LANES)
        out_ref[d] = x.T[: out_ref.shape[1]].astype(BF16)
        return 0

    lax.fori_loop(0, peers, send, 0, unroll=UNROLL)


def stripe(received, weight, bias, taps, lepe_bias, per, qb, first, n_seq, keep=HALF):
    peers = received.shape[0]
    length = peers * per
    return pl.pallas_call(
        functools.partial(stripe_kernel, first, n_seq, per, qb),
        out_shape=jax.ShapeDtypeStruct((peers, keep, n_seq * per), BF16),
        in_specs=[VMEM] * 5,
        out_specs=VMEM,
        scratch_shapes=[
            pltpu.VMEM((n_seq, length, LANES), BF16),
            pltpu.VMEM((n_seq, length, LANES), BF16),
            pltpu.VMEM((n_seq, HEADS, 32, length), BF16),
            pltpu.VMEM((n_seq, length + 16, LANES), F32),
            pltpu.VMEM((n_seq, length, LANES), F32),
        ],
        compiler_params=pltpu.CompilerParams(vmem_limit_bytes=44 * 2**20),
        cost_estimate=pl.CostEstimate(
            flops=4 * HEADS * n_seq * length * length * 256,
            bytes_accessed=4 * 10**6,
            transcendentals=HEADS * n_seq * length * length,
        ),
        name="stripe",
    )(received, weight, bias, taps, lepe_bias)


def tail_kernel(cuts, x_ref, row_ref, *refs):
    cols = refs[: len(cuts)]
    (eye_ref, wr_ref, wc_ref, vec_ref, f1_ref, f1b_ref, f2_ref, out_ref, col_s) = refs[len(cuts) :]
    rows, chans, tile_w = x_ref.shape
    each = row_ref.shape[2] // tile_w
    peers = cols[0].shape[0]
    tile_h = rows * pl.num_programs(0)
    per = tile_w // peers

    @pl.when(pl.program_id(0) == 0)
    def _():
        for (first, count), col_ref in zip(cuts, cols):
            for p in range(peers):
                y = lax.dot_general(col_ref[p], eye_ref[...], TN, preferred_element_type=F32)
                for j in range(count):
                    dst = pl.ds(p * per + first + j, tile_h, stride=tile_w)
                    col_s[dst, :] = y[j * tile_h : (j + 1) * tile_h]

    pb, gain, bias, f2b = [columns(vec_ref[i : i + 1], tile_w) for i in range(4)]
    resids, turned = [], []
    count = rows * tile_w
    both = col_s[pl.ds(pl.multiple_of(pl.program_id(0) * count, count), count), :].astype(BF16)
    for i in range(rows):
        col = both[i * tile_w : (i + 1) * tile_w]
        row = row_ref[i // each][:HALF, i % each * tile_w : (i % each + 1) * tile_w]
        resid = (
            x_ref[i].astype(F32)
            + jnp.dot(wr_ref[...], row, preferred_element_type=F32)
            + lax.dot_general(wc_ref[...], col, NT, preferred_element_type=F32)
            + pb
        )
        turned.append(norm_channels(resid, gain, bias).T.astype(BF16))
        resids.append(resid + f2b)
    normed = jnp.concatenate(turned, axis=0)
    hidden = jnp.dot(normed, f1_ref[...], preferred_element_type=F32) + f1b_ref[...]
    hidden = (0.5 * hidden * (1.0 + lax.erf(hidden * (0.5**0.5)))).astype(BF16)
    out = jnp.dot(hidden, f2_ref[...], preferred_element_type=F32)
    for i in range(rows):
        piece = out[i * tile_w : (i + 1) * tile_w].T
        out_ref[i] = (resids[i] + piece).astype(BF16)


def tail(tokens, row, cuts, cols, proj_w, proj_b, gain, bias, fc1_w, fc1_b, fc2_w, fc2_b):
    tile_h, chans, tile_w = tokens.shape
    each = row.shape[2] // tile_w
    rows = 16 if 16 % each == 0 else each
    ffn = fc1_w.shape[1]
    full = lambda a: pl.BlockSpec(a.shape, lambda i: (0,) * a.ndim)
    block = lambda d: pl.BlockSpec((rows, d, tile_w), lambda i: (i, 0, 0))
    proj_t = proj_w.T
    consts = [
        jnp.eye(HALF, LANES, dtype=BF16), proj_t[:, :HALF],
        jnp.pad(proj_t[:, HALF:], ((0, 0), (0, LANES - HALF))),
        jnp.stack([proj_b, gain, bias, fc2_b]), fc1_w, fc1_b[None], fc2_w,
    ]
    return pl.pallas_call(
        functools.partial(tail_kernel, cuts),
        grid=(tile_h // rows,),
        out_shape=jax.ShapeDtypeStruct(tokens.shape, BF16),
        in_specs=[block(chans), pl.BlockSpec((rows // each,) + row.shape[1:], lambda i: (i, 0, 0))]
        + [full(a) for a in cols] + [full(a) for a in consts],
        out_specs=block(chans),
        scratch_shapes=[pltpu.VMEM((tile_h * tile_w, LANES), F32)],
        compiler_params=pltpu.CompilerParams(vmem_limit_bytes=44 * 2**20),
        cost_estimate=pl.CostEstimate(
            flops=2 * tile_h * tile_w * chans * (chans + 2 * ffn),
            bytes_accessed=8 * 10**6,
            transcendentals=tile_h * tile_w * ffn,
        ),
        name="tail",
    )(tokens, row, *cols, *consts)


def shards(
    tokens, norm1_gain, norm1_bias, qkv_weight, qkv_bias, lepe_taps, lepe_bias, proj_weight,
    proj_bias, norm2_gain, norm2_bias, fc1_weight, fc1_bias, fc2_weight, fc2_bias,
):
    tokens = jnp.swapaxes(tokens, 1, 2)
    tile_h, chans, tile_w = tokens.shape
    n_rows = lax.axis_size("rows")
    n_cols = lax.axis_size("cols")

    def branch(which):
        lo = which * HALF
        lanes = lambda a: jnp.pad(a, [(0, 0)] * (a.ndim - 1) + [(0, LANES - HALF)])
        cut = lambda a: jnp.concatenate(
            [lanes(a[..., b * chans + lo : b * chans + lo + HALF]) for b in range(3)], axis=-1
        )
        return (
            cut(qkv_weight),
            cut(qkv_bias)[None],
            lanes(lepe_taps[:, lo : lo + HALF]),
            lanes(lepe_bias[lo : lo + HALF])[None],
        )

    swap = lambda a, axis: lax.all_to_all(a, axis, split_axis=0, concat_axis=0, tiled=True)
    norm1 = (tokens, norm1_gain, norm1_bias)
    turned = [pltpu.VMEM((tile_w, tile_h, 2 * LANES), F32)]
    col_in = swap(pack(pack_cols_kernel, turned, "pack_cols", *norm1, n_rows), "rows")
    row_out = pack(pack_rows_kernel, [], "pack_rows", *norm1, n_cols)
    row_out, col_in = lax.optimization_barrier((row_out, col_in))
    row_in = swap(row_out, "cols")
    cuts = ((0, tile_w // n_rows),)
    cols = [stripe(col_in, *branch(1), tile_h, n_rows * tile_h, *cut) for cut in cuts]
    cols, row_in = lax.optimization_barrier((cols, row_in))
    cols = [swap(part, "rows") for part in cols]
    rows = stripe(row_in, *branch(0), tile_w, n_cols * tile_w // 2, 0, tile_h // n_cols, 80)
    rows, cols = lax.optimization_barrier((rows, cols))
    rows = swap_blocks(rows, "cols", 1)
    out = tail(
        tokens, rows, cuts, cols, proj_weight, proj_bias, norm2_gain, norm2_bias,
        fc1_weight, fc1_bias, fc2_weight, fc2_bias,
    )
    return jnp.swapaxes(out, 1, 2)


def solution(mesh):
    in_specs = (P("rows", "cols", None),) + (P(),) * 14
    return jax.shard_map(
        shards, mesh=mesh, in_specs=in_specs, out_specs=P("rows", "cols", None), check_vma=False
    )
```
